128 devices in a mesh: rep: 8 (over x_hi, z), shard: 16 (over y, x_lo, core).
Axes of the slice: x: 4 (x_hi: 2, x_lo: 2; x = x_hi * 2 + x_lo), y: 4, z: 4, core: 2. Of those that a mesh axis runs over, the one named last changes fastest.
Arguments:
- hidden: bfloat16 [131072, 1536], P(('rep', 'shard')), may hold values from -24 to 24
- out_grad: bfloat16 [131072, 5120], P(('rep', 'shard')), may hold values from -0.046875 to 0.046875
- inner_params: float32 [8, 1536, 5120], P('rep', 'shard'), may hold values from -4.8 to 4.8
- first_moment: bfloat16 [8, 1536, 5120], P('rep', 'shard'), may hold values from -6 to 6
- second_moment: bfloat16 [8, 1536, 5120], P('rep', 'shard'), may hold values from 0.25 to 4
- anchor: float32 [1536, 5120], P('shard'), may hold values from -4 to 4
- outer_moment: float32 [1536, 5120], P('shard', 'rep'), may hold values from -0.6 to 0.6
Outputs:
- new_params: float32 [1536, 5120], P('shard')
- new_first: bfloat16 [8, 1536, 5120], P('rep', 'shard')
- new_second: bfloat16 [8, 1536, 5120], P('rep', 'shard')
- new_moment: float32 [1536, 5120], P('shard', 'rep')
The draws below stay inside these ranges and needn't reach their ends.
All inputs are finite; a program needn't handle non-finite values.
Results may differ from the reference program's by a relative error of at most 0.012.
Values may be sent and summed in bfloat16 or wider, within the bound.
No kernel may reach another device: no remote copies, remote signals or barrier semaphores. Data moves between devices by JAX's collectives and lax.ppermute only.
A program may use at most 128 MiB of HBM per device.

```python
import math
import jax
import jax.numpy as jnp
from jax import lax

D = 5120
FF = 1536
TOK_DEV = 1024
REPLICAS = 8
TOKENS = 131072
N_SHARD = 16


def anchor_field(key):
    return jax.random.truncated_normal(key, -4.0, 4.0, (FF, D), jnp.float32)


def draw_anchor(key, part):
    shared = anchor_field(key)
    return shared


def draw_inner_params(key, part):
    shared = anchor_field(key)
    key = jax.random.fold_in(key, 12)
    own_key = jax.random.fold_in(key, 0)
    drift = 0.2 * jax.random.truncated_normal(own_key, -4.0, 4.0, (REPLICAS, FF, D), jnp.float32)
    return shared[None] + drift


def strengthened(drawn, key, source, target, blocks, factor):
    def block_of(position):
        return (jnp.arange(drawn.shape[position]) // (drawn.shape[position] // blocks)).reshape((-1,) + (1,) * (drawn.ndim - 1 - position))

    first = jax.random.permutation(key, blocks)[block_of(target)]
    second = (block_of(target) + blocks // 2) % blocks
    return jnp.where((block_of(source) == first) | (block_of(source) == second), factor * drawn, drawn)


def level_of(key, dims, cuts, smallest, high):
    level = 1.0
    for axis_at, parts in cuts:
        draws = jax.random.uniform(jax.random.fold_in(jax.random.fold_in(key, 6), axis_at), (parts,), jnp.float32, smallest / len(cuts), high / len(cuts))
        level = level * jnp.repeat(jnp.exp(draws), dims[axis_at] // parts).reshape((-1,) + (1,) * (len(dims) - 1 - axis_at))
    return level


def centred(key, dims, scale, limit, cuts=(), kind=jnp.bfloat16):
    values = scale * jax.random.normal(key, dims, jnp.float32)
    if cuts:
        values = values * level_of(key, dims, cuts, -0.22, 0.18)
    return jnp.clip(values, -limit, limit).astype(kind)


def noise_with(key, dims, deviation, bound, cuts, heavy, held_as=jnp.bfloat16):
    array = deviation * jax.random.normal(key, dims, jnp.float32)
    if cuts:
        array = array * level_of(key, dims, cuts, -0.22, 0.18)
    return jnp.clip(strengthened(array, jax.random.fold_in(key, 3), *heavy), -bound, bound).astype(held_as)


def setup_inputs(seed: int = 0) -> dict:
    keys = jax.random.split(jax.random.key(seed), 8)
    hidden = noise_with(keys[0], (TOKENS, FF), 1.0, 24.0, ((0, 128),), (0, 1, 128, 5.5))
    out_grad = centred(keys[1], (TOKENS, D), (TOK_DEV * N_SHARD) ** -0.5, 0.046875, ((0, 128),))
    inner_params = draw_inner_params(jax.random.fold_in(keys[7], 71), 0)
    first_moment = centred(keys[3], (REPLICAS, FF, D), 1.0, 6.0, ((0, 8), (1, 16)))
    second_moment = jnp.clip(jnp.exp(math.log(4.0) - 2.7725887 * jax.random.uniform(keys[4], (REPLICAS, FF, D), jnp.float32) ** level_of(keys[4], (REPLICAS, FF, D), ((0, 8), (1, 16)), -0.2, 0.2)), 0.25, 4.0).astype(jnp.bfloat16)
    anchor = draw_anchor(jax.random.fold_in(keys[7], 71), 0)
    outer_moment = centred(keys[6], (FF, D), 0.1, 0.6, ((0, 16), (1, 8)), jnp.float32)
    return dict(hidden=hidden, out_grad=out_grad, inner_params=inner_params, first_moment=first_moment, second_moment=second_moment, anchor=anchor, outer_moment=outer_moment)


beta_first = 0.9
beta_second = 0.95
bias_first = 1.0 - 0.9 ** 30
bias_second = 1.0 - 0.95 ** 30
inner_rate = 0.05
decay_rate = 0.1
epsilon = 1e-08
outer_beta = 0.9
outer_rate = 0.7

def adam_rows(gradient, first_rows, second_rows, param_rows):
    first_fresh = beta_first * first_rows.astype(jnp.float32) + (1.0 - beta_first) * gradient
    second_fresh = beta_second * second_rows.astype(jnp.float32) + (1.0 - beta_second) * gradient * gradient
    update = first_fresh / bias_first / (jnp.sqrt(second_fresh / bias_second) + epsilon) + decay_rate * param_rows
    stepped = param_rows - inner_rate * update
    return (first_fresh, second_fresh, stepped)

def reference(hidden, out_grad, inner_params, first_moment, second_moment, anchor, outer_moment):
    hidden_blocks = hidden.reshape(REPLICAS, N_SHARD, TOK_DEV, FF)
    grad_blocks = out_grad.reshape(REPLICAS, N_SHARD, TOK_DEV, D)

    def replica_gradient(blocks_pair):

        def add_partial(running, shard_pair):
            partial_value = jnp.dot(shard_pair[0].T, shard_pair[1], preferred_element_type=jnp.float32)
            rounded = lax.optimization_barrier(partial_value.astype(jnp.bfloat16))
            return (running + rounded.astype(jnp.float32), None)
        return lax.scan(add_partial, jnp.zeros((FF, D), jnp.float32), blocks_pair)[0]
    gradient = lax.map(replica_gradient, (hidden_blocks, grad_blocks))
    first_fresh, second_fresh, stepped = adam_rows(gradient, first_moment, second_moment, inner_params)
    pseudo = lax.optimization_barrier(jnp.sum(anchor[None] - stepped, axis=0)) / REPLICAS
    moment_new = outer_beta * outer_moment + pseudo
    params_new = anchor - outer_rate * (pseudo + outer_beta * moment_new)
    return (params_new, first_fresh.astype(jnp.bfloat16), second_fresh.astype(jnp.bfloat16), moment_new)
```

```python
import functools

import jax
import jax.numpy as jnp
from jax import lax
from jax.experimental import pallas as pl
from jax.experimental.pallas import tpu as pltpu
from jax.sharding import PartitionSpec as P

beta_first = 0.9
beta_second = 0.95
bias_first = 1.0 - 0.9**30
bias_second = 1.0 - 0.95**30
inner_rate = 0.05
decay_rate = 0.1
epsilon = 1e-08
outer_beta = 0.9
outer_rate = 0.7

pseudo_weight = 1.0 + outer_beta
moment_weight = outer_beta * outer_beta

SHARDS = 16
REPLICAS = 8
BF = jnp.bfloat16
F32 = jnp.float32
LIMIT = 40 * 1024 * 1024

CORE = 1
MASKS = (2, 4, 12)
CHUNKS = (
    (0, 1792, (0, 1, 2)),
    (1792, 1792, (1, 2, 0)),
    (3584, 1536, (2, 0, 1)),
)
GROUPS = ((0,), (1, 2))
TILE = 256


def swap(value, mask):
    return lax.ppermute(value, "shard", [(i, i ^ mask) for i in range(SHARDS)])


def swap_rep(value, mask):
    return lax.ppermute(value, "rep", [(i, i ^ mask) for i in range(REPLICAS)])


def params(**kw):
    return pltpu.CompilerParams(vmem_limit_bytes=LIMIT, **kw)


def turn_kernel(rows, place, hidden_ref, own_ref, other_ref, turned):
    turned[...] = hidden_ref[...].T.reshape(turned.shape)
    me = place[0]
    for bx in range(2):
        for ba in range(2):
            for bb in range(2):
                mask = (bx * MASKS[0]) ^ (ba * MASKS[1]) ^ (bb * MASKS[2])
                own_ref[bx, ba, bb] = turned[me ^ mask]
                other_ref[bx, ba, bb] = turned[me ^ mask ^ CORE]


def turn(hidden, place):
    tokens, width = hidden.shape
    rows = width // SHARDS
    step = min(256, tokens)
    shape = jax.ShapeDtypeStruct((2, 2, 2, rows, tokens), BF)
    block = pl.BlockSpec((2, 2, 2, rows, step), lambda i, p: (0, 0, 0, 0, i))
    return pl.pallas_call(
        functools.partial(turn_kernel, rows),
        grid_spec=pltpu.PrefetchScalarGridSpec(
            num_scalar_prefetch=1,
            grid=(tokens // step,),
            in_specs=[pl.BlockSpec((step, width), lambda i, p: (i, 0))],
            out_specs=[block, block],
            scratch_shapes=[pltpu.VMEM((SHARDS, rows, step), BF)],
        ),
        out_shape=[shape, shape],
        compiler_params=params(),
        cost_estimate=pl.CostEstimate(flops=0, bytes_accessed=4 * tokens * width, transcendentals=0),
        name="turn",
    )(place, hidden)


def product_kernel(left_ref, left_far_ref, right_ref, right_far_ref, out_ref):
    depth = left_ref.shape[-1]
    left = left_ref[...].reshape(-1, depth)
    left_far = left_far_ref[...].reshape(-1, depth)
    total = jnp.dot(left, right_ref[...], preferred_element_type=F32)
    total += jnp.dot(left_far, right_far_ref[...], preferred_element_type=F32)
    out_ref[...] = total.astype(BF).reshape(out_ref.shape)


def product(left, left_far, right, right_far, dim, bit, first, width):
    rows, depth = left.shape[3:]
    halves = [2, 2, 2]
    halves[dim] = 1
    place = [0, 0, 0]
    place[dim] = bit
    lhs = pl.BlockSpec((*halves, rows, depth), lambda i: (*place, 0, 0))
    flops = 2 * 2 * 4 * rows * depth * width
    return pl.pallas_call(
        product_kernel,
        grid=(width // TILE,),
        in_specs=[
            lhs,
            lhs,
            pl.BlockSpec((depth, TILE), lambda i: (0, first // TILE + i)),
            pl.BlockSpec((depth, TILE), lambda i: (0, i)),
        ],
        out_specs=pl.BlockSpec((2, 2, rows, TILE), lambda i: (0, 0, 0, i)),
        out_shape=jax.ShapeDtypeStruct((2, 2, rows, width), BF),
        compiler_params=params(),
        cost_estimate=pl.CostEstimate(
            flops=flops,
            bytes_accessed=2 * (4 * depth * rows * 2 + 2 * depth * width + 4 * rows * width),
            transcendentals=0,
        ),
        name="product",
    )(left, left_far, right, right_far)


def adam_kernel(chained, place, *refs):
    grads, rest = refs[:2], refs[2:]
    first_ref, second_ref, param_ref, anchor_ref, moment_ref = rest[:5]
    outs = rest[5 + chained :]
    first_out, second_out = outs[:2]
    parts = outs[2:6]
    quarters = outs[6]
    gradient = grads[0][...].astype(F32) + grads[1][...].astype(F32)
    first_fresh = beta_first * first_ref[0].astype(F32) + (1.0 - beta_first) * gradient
    second_fresh = beta_second * second_ref[0].astype(F32) + (1.0 - beta_second) * gradient * gradient
    rows = param_ref[0]
    update = first_fresh / bias_first / (jnp.sqrt(second_fresh / bias_second) + epsilon) + decay_rate * rows
    stepped = rows - inner_rate * update
    first_out[0] = first_fresh.astype(BF)
    second_out[0] = second_fresh.astype(BF)
    departure = (anchor_ref[...] - stepped) * (pseudo_weight / REPLICAS) + moment_ref[...]
    quarters[...] = departure.reshape(quarters.shape)
    for distance in range(4):
        parts[distance][...] = quarters[place[1] ^ distance].astype(BF)


def adam(place, grads, first, second, param, anchor, moment, column, width, before, group_column, group_width):
    rows, total_width = anchor.shape
    step = TILE
    part = rows // 4

    def at(offset):
        return lambda i, p: (0, offset // step + i)

    def at3(offset):
        return lambda i, p: (0, 0, offset // step + i)

    flat = pl.BlockSpec((rows, step), at(column))
    deep = pl.BlockSpec((1, rows, step), at3(column))
    part_spec = pl.BlockSpec((part, step), at(group_column))
    part_shape = jax.ShapeDtypeStruct((part, group_width), BF)
    firsts, seconds, parts = before
    chain = [(0, firsts), (1, seconds)] + [(2 + d, p) for d, p in enumerate(parts or ())]
    chain = [(o, a) for o, a in chain if a is not None]
    aliases = {1 + 7 + n: o for n, (o, _) in enumerate(chain)}
    outs = pl.pallas_call(
        functools.partial(adam_kernel, len(chain)),
        grid_spec=pltpu.PrefetchScalarGridSpec(
            num_scalar_prefetch=1,
            grid=(width // step,),
            in_specs=[pl.BlockSpec((rows, step), at(0))] * 2
            + [deep, deep, deep, flat, flat]
            + [pl.BlockSpec(memory_space=pl.ANY)] * len(chain),
            out_specs=[deep, deep] + [part_spec] * 4,
            scratch_shapes=[pltpu.VMEM((4, part, step), F32)],
        ),
        out_shape=[jax.ShapeDtypeStruct(first.shape, BF)] * 2 + [part_shape] * 4,
        input_output_aliases=aliases,
        compiler_params=params(),
        cost_estimate=pl.CostEstimate(flops=20 * rows * width, bytes_accessed=24 * rows * width, transcendentals=0),
        name="adam",
    )(place, *grads, first, second, param, anchor, moment, *(a for _, a in chain))
    return outs[0], outs[1], outs[2:]


def last_kernel(chained, place, p0, p1, p2, p3, anchor_ref, *refs):
    params_out, total_out, quarters = refs[chained:]
    for distance, piece in enumerate((p0, p1, p2, p3)):
        quarters[place[1] ^ distance] = piece[...].astype(F32)
    total = quarters[...].reshape(anchor_ref.shape)
    params_out[...] = anchor_ref[...] - outer_rate * total
    total_out[...] = total


def last(place, pieces, anchor, column, width, before):
    rows, total_width = anchor.shape
    part = rows // 4
    step = TILE
    piece = pl.BlockSpec((part, step), lambda i, p: (0, i))
    flat = pl.BlockSpec((rows, step), lambda i, p: (0, column // step + i))
    shape = jax.ShapeDtypeStruct(anchor.shape, F32)
    chain = [a for a in before if a is not None]
    return pl.pallas_call(
        functools.partial(last_kernel, len(chain)),
        grid_spec=pltpu.PrefetchScalarGridSpec(
            num_scalar_prefetch=1,
            grid=(width // step,),
            in_specs=[piece] * 4 + [flat] + [pl.BlockSpec(memory_space=pl.ANY)] * len(chain),
            out_specs=[flat, flat],
            scratch_shapes=[pltpu.VMEM((4, part, step), F32)],
        ),
        out_shape=[shape, shape],
        input_output_aliases={6 + n: n for n in range(len(chain))},
        compiler_params=params(),
        cost_estimate=pl.CostEstimate(flops=2 * rows * width, bytes_accessed=14 * rows * width, transcendentals=0),
        name="last",
    )(place, *pieces, anchor, *chain)


def add(*values):
    total = values[0].astype(F32)
    for value in values[1:]:
        total = total + value.astype(F32)
    return total.astype(BF)


def body(hidden, out_grad, inner_params, first_moment, second_moment, anchor, outer_moment):
    me = lax.axis_index("shard")
    rep = lax.axis_index("rep")
    share = outer_moment.shape[1]
    place = jnp.stack([me, rep % 4]).astype(jnp.int32)
    placed_moment = lax.dynamic_update_slice(
        jnp.zeros(anchor.shape, F32), moment_weight * outer_moment, (0, rep * share)
    )

    own, other = turn(hidden, place)
    far = swap(other, CORE)
    grads_far = [swap(out_grad[:, c : c + w], CORE) for c, w, _ in CHUNKS]

    arrived = []
    for (column, width, order), grad_far in zip(CHUNKS, grads_far):
        sent = product(own, far, out_grad, grad_far, order[0], 1, column, width)
        arrived.append(swap(sent, MASKS[order[0]]))
    kept = []
    for (column, width, order), grad_far in zip(CHUNKS, grads_far):
        kept.append(product(own, far, out_grad, grad_far, order[0], 0, column, width))
    seconds = []
    for (column, width, order), mine, came in zip(CHUNKS, kept, arrived):
        if order[1] == min(order[1:]):
            go = add(mine[1], came[1])
            stay = add(mine[0], came[0])
        else:
            go = add(mine[:, 1], came[:, 1])
            stay = add(mine[:, 0], came[:, 0])
        seconds.append((stay, swap(go, MASKS[order[1]])))
    thirds = []
    for (column, width, order), (mine, came) in zip(CHUNKS, seconds):
        go = add(mine[1], came[1])
        stay = add(mine[0], came[0])
        thirds.append((stay, swap(go, MASKS[order[2]])))

    firsts = secs = None
    result = [None, None]
    for group in GROUPS:
        group_column = CHUNKS[group[0]][0]
        group_width = sum(CHUNKS[n][1] for n in group)
        parts = None
        for n in group:
            column, width, _ = CHUNKS[n]
            firsts, secs, parts = adam(
                place, thirds[n], first_moment, second_moment, inner_params, anchor, placed_moment,
                column, width, (firsts, secs, parts), column - group_column, group_width,
            )
        mine = add(parts[0], *(swap_rep(parts[d], d) for d in (1, 3, 2)))
        mine = add(mine, swap_rep(mine, 4))
        pieces = [mine] + [swap_rep(mine, d) for d in (1, 2, 3)]
        result = last(place, pieces, anchor, group_column, group_width, result)
    params_new, total = result
    total_share = lax.dynamic_slice_in_dim(total, rep * share, share, 1)
    moment_new = outer_beta * outer_moment + (total_share - moment_weight * outer_moment) / pseudo_weight
    return (params_new, firsts, secs, moment_new)


def solution(mesh):
    placed = (
        P(("rep", "shard"), None),
        P(("rep", "shard"), None),
        P("rep", "shard", None),
        P("rep", "shard", None),
        P("rep", "shard", None),
        P("shard", None),
        P("shard", "rep"),
    )
    return jax.shard_map(
        body,
        mesh=mesh,
        in_specs=placed,
        out_specs=(
            P("shard", None),
            P("rep", "shard", None),
            P("rep", "shard", None),
            P("shard", "rep"),
        ),
        check_vma=False,
    )
```

```python
import functools

import jax
import jax.numpy as jnp
from jax import lax
from jax.experimental import pallas as pl
from jax.experimental.pallas import tpu as pltpu
from jax.sharding import PartitionSpec as P

beta_first = 0.9
beta_second = 0.95
bias_first = 1.0 - 0.9**30
bias_second = 1.0 - 0.95**30
inner_rate = 0.05
decay_rate = 0.1
epsilon = 1e-08
outer_beta = 0.9
outer_rate = 0.7

pseudo_weight = 1.0 + outer_beta
moment_weight = outer_beta * outer_beta

SHARDS = 16
REPLICAS = 8
BF = jnp.bfloat16
F32 = jnp.float32
LIMIT = 20 * 1024 * 1024
LIGHT = pl.CostEstimate(flops=0, bytes_accessed=1024, transcendentals=0)

CORE = 1
MASKS = (2, 4, 12)
CHUNKS = (
    (0, 1792, (0, 1, 2)),
    (1792, 1792, (1, 2, 0)),
    (3584, 1536, (2, 0, 1)),
)
GROUPS = ((0, 1), (2,))
PLAN = (
    *(("other", n) for n in range(3)),
    *(("send", n) for n in range(3)),
    *(("keep", n) for n in range(3)),
    ("hold", 0),
    *(("fold", n) for n in range(3)),
    *(("again", n) for n in range(3)),
    *(("adam", n) for n in range(3)),
    *((kind, n) for kind in ("sum", "total", "last") for n in range(2)),
)


def swap(value, mask):
    return lax.ppermute(value, "shard", [(i, i ^ mask) for i in range(SHARDS)])


def swap_rep(value, mask):
    return lax.ppermute(value, "rep", [(i, i ^ mask) for i in range(REPLICAS)])


def params(**kw):
    return pltpu.CompilerParams(vmem_limit_bytes=LIMIT, **kw)


def turn_kernel(place, hidden_ref, grad_ref, own_ref, other_ref, held_ref, landed, turned, sems, grad_sems):
    count, step, _ = landed.shape
    strip = grad_ref.shape[0] // count

    def fetch(n):
        return pltpu.make_async_copy(hidden_ref.at[pl.ds(n * step, step)], landed.at[n], sems.at[n])

    def hold(n):
        rows = pl.ds(n * strip, strip)
        return pltpu.make_async_copy(grad_ref.at[rows], held_ref.at[rows], grad_sems.at[n])

    for n in range(count):
        fetch(n).start()
    for n in range(count):
        hold(n).start()
    me = place[0]
    for n in range(count):
        fetch(n).wait()
        turned[...] = landed[n].T.reshape(turned.shape)
        tokens = slice(n * step, (n + 1) * step)
        for bx in range(2):
            for ba in range(2):
                for bb in range(2):
                    mask = (bx * MASKS[0]) ^ (ba * MASKS[1]) ^ (bb * MASKS[2])
                    own_ref[bx, ba, bb, :, tokens] = turned[me ^ mask]
                    other_ref[bx, ba, bb, :, tokens] = turned[me ^ mask ^ CORE]
    for n in range(count):
        hold(n).wait()


def in_vmem(value):
    return pltpu.with_memory_space_constraint(value, pltpu.VMEM)


def in_hbm(value):
    return pltpu.with_memory_space_constraint(value, pltpu.HBM)


WHOLE = pl.BlockSpec(memory_space=pltpu.VMEM)
SCALARS = pl.BlockSpec(memory_space=pltpu.SMEM)


def turn(hidden, out_grad, place):
    tokens, width = hidden.shape
    rows = width // SHARDS
    step = min(256, tokens)
    steps = tokens // step
    shape = pltpu.VMEM((2, 2, 2, rows, tokens), BF)
    far = pl.BlockSpec(memory_space=pltpu.HBM)
    return pl.pallas_call(
        turn_kernel,
        in_specs=[SCALARS, far, far],
        out_specs=[WHOLE] * 3,
        scratch_shapes=[
            pltpu.VMEM((steps, step, width), BF),
            pltpu.VMEM((SHARDS, rows, step), BF),
            pltpu.SemaphoreType.DMA((steps,)),
            pltpu.SemaphoreType.DMA((steps,)),
        ],
        out_shape=[shape, shape, pltpu.VMEM(out_grad.shape, BF)],
        compiler_params=params(),
        cost_estimate=LIGHT,
        name="turn",
    )(place, in_hbm(hidden), in_hbm(out_grad))


def product_kernel(added, spot, turned, first, step, place, left_ref, right_ref, *refs):
    depth = left_ref.shape[-1]
    out_ref = refs[-1]
    left = left_ref[spot].reshape(-1, depth)
    flat = len(out_ref.shape) - 1

    def columns(t, _):
        here = pl.ds(pl.multiple_of(t * step, 128), step)
        total = jnp.dot(left, right_ref[:, pl.ds(pl.multiple_of(first + t * step, 128), step)], preferred_element_type=F32)
        total = total.reshape(*out_ref.shape[:-1], step)
        for n in range(added):
            total += refs[n][(*spot, slice(None), here)].astype(F32)
        total = total.astype(BF)
        if turned:
            for p in range(2):
                for q in range(2):
                    out_ref[q, p, :, here] = total[p, q]
        else:
            out_ref[(*(slice(None),) * flat, here)] = total
        return 0

    lax.fori_loop(0, out_ref.shape[-1] // step, columns, 0)


def product(place, left, right, first, width, order=None, bit=0, add=None):
    rows = left.shape[3]
    dim = order[0] if order else None
    turned = bool(order) and order[1] > order[2]
    spot = tuple(bit if d == dim else slice(None) for d in range(3))
    kept = (2,) * (3 if dim is None else 2)
    args = [left, right] + ([] if add is None else [add])
    return pl.pallas_call(
        functools.partial(product_kernel, int(add is not None), spot, turned, first, width // 2),
        in_specs=[SCALARS] + [WHOLE] * len(args),
        out_specs=WHOLE,
        out_shape=pltpu.VMEM((*kept, rows, width), BF),
        compiler_params=params(),
        cost_estimate=LIGHT,
        name="product",
    )(place, *(in_vmem(a) for a in args))


def adam_kernel(chained, column, group_column, place, *refs):
    mine_ref, came_ref, first_ref, second_ref, param_ref, anchor_ref, moment_ref = refs[:7]
    first_out, second_out = refs[7 + chained : 9 + chained]
    parts = refs[9 + chained : 13 + chained]
    quarters = refs[13 + chained]
    step = quarters.shape[-1]

    def columns(t, _):
        near = pl.ds(pl.multiple_of(t * step, 128), step)
        here = pl.ds(pl.multiple_of(column + t * step, 128), step)
        gradient = mine_ref[:, near].astype(F32) + came_ref[:, near].astype(F32)
        first_fresh = beta_first * first_ref[0, :, here].astype(F32) + (1.0 - beta_first) * gradient
        second_fresh = beta_second * second_ref[0, :, here].astype(F32) + (1.0 - beta_second) * gradient * gradient
        level = second_fresh * (1.0 / bias_second)
        root = level * lax.rsqrt(level)
        stepped = (1.0 - inner_rate * decay_rate) * param_ref[0, :, here]
        stepped = stepped - first_fresh * (inner_rate / bias_first) / (root + epsilon)
        first_out[0, :, here] = first_fresh.astype(BF)
        second_out[0, :, here] = second_fresh.astype(BF)
        departure = (anchor_ref[:, here] - stepped) * (pseudo_weight / REPLICAS) + moment_ref[:, here]
        quarters[...] = departure.reshape(quarters.shape)
        wide = pl.ds(pl.multiple_of(group_column + t * step, 128), step)
        for distance in range(4):
            parts[distance][:, wide] = quarters[place[1] ^ distance].astype(BF)
        return 0

    lax.fori_loop(0, mine_ref.shape[-1] // step, columns, 0)


def adam(place, grads, first, second, param, anchor, moment, column, width, before, group_column, group_width):
    rows, total_width = anchor.shape
    part = rows // 4
    part_shape = pltpu.VMEM((part, group_width), BF)
    firsts, seconds, parts = before
    chain = [(0, firsts), (1, seconds)] + [(2 + d, p) for d, p in enumerate(parts or ())]
    chain = [(o, a) for o, a in chain if a is not None]
    outs = pl.pallas_call(
        functools.partial(adam_kernel, len(chain), column, group_column),
        in_specs=[SCALARS] + [WHOLE] * (7 + len(chain)),
        out_specs=[WHOLE] * 6,
        scratch_shapes=[pltpu.VMEM((4, part, 128), F32)],
        out_shape=[pltpu.VMEM(first.shape, BF)] * 2 + [part_shape] * 4,
        input_output_aliases={8 + n: o for n, (o, _) in enumerate(chain)},
        compiler_params=params(),
        cost_estimate=LIGHT,
        name="adam",
    )(place, *(in_vmem(a) for a in (*grads, first, second, param, anchor, moment)), *(in_vmem(a) for _, a in chain))
    return outs[0], outs[1], outs[2:]


def hold_kernel(place, first, second, param, anchor, moment, *refs):
    outs, sems = refs[:5], refs[6]
    share_ref = refs[5]
    copies = [
        pltpu.make_async_copy(source, target, sems.at[n])
        for n, (source, target) in enumerate(zip((first, second, param, anchor, moment), (*outs[:4], share_ref)))
    ]
    for copy in copies:
        copy.start()
    placed = outs[4]
    width = share_ref.shape[1]
    placed[...] = jnp.zeros_like(placed)
    copies[4].wait()
    placed[:, pl.ds(pl.multiple_of(place[2] * width, 128), width)] = moment_weight * share_ref[...]
    for copy in copies[:4]:
        copy.wait()


def hold(place, first, second, param, anchor, moment):
    far = pl.BlockSpec(memory_space=pltpu.HBM)
    args = (first, second, param, anchor, moment)
    return pl.pallas_call(
        hold_kernel,
        in_specs=[SCALARS] + [far] * 5,
        out_specs=[WHOLE] * 5,
        out_shape=[pltpu.VMEM(a.shape, a.dtype) for a in args[:4]] + [pltpu.VMEM(anchor.shape, F32)],
        scratch_shapes=[pltpu.VMEM(moment.shape, F32), pltpu.SemaphoreType.DMA((5,))],
        compiler_params=params(),
        cost_estimate=LIGHT,
        name="hold",
    )(place, *(in_hbm(a) for a in args))


def last_kernel(chained, column, place, p0, p1, p2, p3, anchor_ref, *refs):
    params_out, total_out, fresh, quarters, sem = refs[chained:]
    step = quarters.shape[-1]

    def columns(t, _):
        near = pl.ds(pl.multiple_of(t * step, 128), step)
        here = pl.ds(pl.multiple_of(column + t * step, 128), step)
        for distance, piece in enumerate((p0, p1, p2, p3)):
            quarters[place[1] ^ distance] = piece[:, near].astype(F32)
        total = quarters[...].reshape(-1, step)
        fresh[:, near] = anchor_ref[:, here] - outer_rate * total
        total_out[:, here] = total.astype(BF)
        return 0

    lax.fori_loop(0, fresh.shape[-1] // step, columns, 0)
    copy = pltpu.make_async_copy(fresh, params_out.at[:, pl.ds(column, fresh.shape[-1])], sem)
    copy.start()
    copy.wait()


def last(place, pieces, anchor, column, width, before):
    rows = anchor.shape[0]
    chain = [a for a in before if a is not None]
    if chain:
        chain = [in_hbm(chain[0]), in_vmem(chain[1])]
    far = pl.BlockSpec(memory_space=pltpu.HBM)
    return pl.pallas_call(
        functools.partial(last_kernel, len(chain), column),
        in_specs=[SCALARS] + [WHOLE] * 5 + [far, WHOLE][: len(chain)],
        out_specs=[far, WHOLE],
        out_shape=[pltpu.HBM(anchor.shape, F32), pltpu.VMEM(anchor.shape, BF)],
        scratch_shapes=[
            pltpu.VMEM((rows, width), F32),
            pltpu.VMEM((4, rows // 4, 128), F32),
            pltpu.SemaphoreType.DMA(()),
        ],
        input_output_aliases={6 + n: n for n in range(len(chain))},
        compiler_params=params(),
        cost_estimate=LIGHT,
        name="last",
    )(place, *(in_vmem(p) for p in pieces), in_vmem(anchor), *chain)


def add(*values):
    total = values[0].astype(F32)
    for value in values[1:]:
        total = total + value.astype(F32)
    return total.astype(BF)


def body(hidden, out_grad, inner_params, first_moment, second_moment, anchor, outer_moment):
    me = lax.axis_index("shard")
    rep = lax.axis_index("rep")
    share = outer_moment.shape[1]
    place = jnp.stack([me, rep % 4, rep]).astype(jnp.int32)
    own, other, held = turn(hidden, out_grad, place)
    count = len(CHUNKS)
    across, kept, arrived, twice, thrice = ([None] * count for _ in range(5))
    group_of = {n: g for g, group in enumerate(GROUPS) for n in group}
    parts, sums = [None] * len(GROUPS), [None] * len(GROUPS)
    firsts = seconds = None
    result = [None, None]
    token = place

    for kind, n in PLAN:
        column, width, order = CHUNKS[n]
        if kind == "other":
            done = product(token, other, held, column, width)
            across[n] = swap(done, CORE)
        elif kind == "send":
            done = product(token, own, held, column, width, order, 1, across[n])
            arrived[n] = swap(done, MASKS[order[0]])
        elif kind == "keep":
            done = kept[n] = product(token, own, held, column, width, order, 0, across[n])
        elif kind == "hold":
            first_held, second_held, param_held, anchor_held, moment_held = hold(
                token, first_moment, second_moment, inner_params, anchor, outer_moment
            )
            done = moment_held
        elif kind == "fold":
            mine, token = lax.optimization_barrier((kept[n], token))
            done = add(mine[1], arrived[n][1])
            twice[n] = (add(mine[0], arrived[n][0]), swap(done, MASKS[order[1]]))
        elif kind == "again":
            came = twice[n][1]
            mine, token = lax.optimization_barrier((twice[n][0], token))
            done = add(mine[1], came[1])
            thrice[n] = (add(mine[0], came[0]), swap(done, MASKS[order[2]]))
        elif kind == "adam":
            group = group_of[n]
            group_column = CHUNKS[GROUPS[group][0]][0]
            group_width = sum(CHUNKS[m][1] for m in GROUPS[group])
            firsts, seconds, parts[group] = adam(
                token, thrice[n], first_held, second_held, param_held, anchor_held, moment_held,
                column, width, (firsts, seconds, parts[group]), column - group_column, group_width,
            )
            done = parts[group][0]
            if n == GROUPS[group][-1]:
                parts[group] = [done] + [swap_rep(parts[group][d], d) for d in (1, 2, 3)]
        elif kind == "sum":
            mine, token = lax.optimization_barrier((parts[n][0], token))
            done = add(mine, *parts[n][1:])
            sums[n] = (done, swap_rep(done, 4))
        elif kind == "total":
            mine, token = lax.optimization_barrier((sums[n][0], token))
            done = add(mine, sums[n][1])
            sums[n] = [done] + [swap_rep(done, d) for d in (1, 2, 3)]
        elif kind == "last":
            column = CHUNKS[GROUPS[n][0]][0]
            width = sum(CHUNKS[m][1] for m in GROUPS[n])
            result = last(token, sums[n], anchor_held, column, width, result)
            done = result[1]
        token, _ = lax.optimization_barrier((token, done))
    params_new, total = result
    total_share = lax.dynamic_slice_in_dim(total, rep * share, share, 1).astype(F32)
    moment_new = outer_beta * outer_moment + (total_share - moment_weight * outer_moment) / pseudo_weight
    return (params_new, firsts, seconds, moment_new)


def solution(mesh):
    placed = (
        P(("rep", "shard"), None),
        P(("rep", "shard"), None),
        P("rep", "shard", None),
        P("rep", "shard", None),
        P("rep", "shard", None),
        P("shard", None),
        P("shard", "rep"),
    )
    return jax.shard_map(
        body,
        mesh=mesh,
        in_specs=placed,
        out_specs=(
            P("shard", None),
            P("rep", "shard", None),
            P("rep", "shard", None),
            P("shard", "rep"),
        ),
        check_vma=False,
    )
```

```python
import functools

import jax
import jax.numpy as jnp
from jax import lax
from jax.experimental import pallas as pl
from jax.experimental.pallas import tpu as pltpu
from jax.sharding import PartitionSpec as P

beta_first = 0.9
beta_second = 0.95
bias_first = 1.0 - 0.9**30
bias_second = 1.0 - 0.95**30
inner_rate = 0.05
decay_rate = 0.1
epsilon = 1e-08
outer_beta = 0.9
outer_rate = 0.7

pseudo_weight = 1.0 + outer_beta
moment_weight = outer_beta * outer_beta

SHARDS = 16
REPLICAS = 8
BF = jnp.bfloat16
F32 = jnp.float32
LIMIT = 20 * 1024 * 1024
LIGHT = pl.CostEstimate(flops=0, bytes_accessed=1024, transcendentals=0)

CORE = 1
MASKS = (2, 4, 12)
CHUNKS = (
    (0, 1792, (0, 1, 2)),
    (1792, 1792, (1, 2, 0)),
    (3584, 1536, (2, 0, 1)),
)
GROUPS = ((0, 1), (2,))
PLAN = (
    *(("other", n) for n in range(3)),
    *(("send", n) for n in range(3)),
    *(("keep", n) for n in range(3)),
    ("hold", 0),
    *(("fold", n) for n in range(3)),
    *(("again", n) for n in range(3)),
    *(("adam", n) for n in range(3)),
    ("store", 0),
    *((kind, n) for kind in ("sum", "total", "last") for n in range(2)),
)


def swap(value, mask):
    return lax.ppermute(value, "shard", [(i, i ^ mask) for i in range(SHARDS)])


def swap_rep(value, mask):
    return lax.ppermute(value, "rep", [(i, i ^ mask) for i in range(REPLICAS)])


def params(**kw):
    return pltpu.CompilerParams(vmem_limit_bytes=LIMIT, **kw)


def turn_kernel(place, hidden_ref, grad_ref, own_ref, other_ref, held_ref, landed, turned, sems, grad_sems):
    count, step, _ = landed.shape
    strip = grad_ref.shape[0] // count

    def fetch(n):
        return pltpu.make_async_copy(hidden_ref.at[pl.ds(n * step, step)], landed.at[n], sems.at[n])

    def hold(n):
        rows = pl.ds(n * strip, strip)
        return pltpu.make_async_copy(grad_ref.at[rows, pl.ds(0, held_ref.shape[1])], held_ref.at[rows], grad_sems.at[n])

    for n in range(count):
        fetch(n).start()
    for n in range(count):
        hold(n).start()
    me = place[0]
    for n in range(count):
        fetch(n).wait()
        turned[...] = landed[n].T.reshape(turned.shape)
        tokens = slice(n * step, (n + 1) * step)
        for bx in range(2):
            for ba in range(2):
                for bb in range(2):
                    mask = (bx * MASKS[0]) ^ (ba * MASKS[1]) ^ (bb * MASKS[2])
                    own_ref[bx, ba, bb, :, tokens] = turned[me ^ mask]
                    other_ref[bx, ba, bb, :, tokens] = turned[me ^ mask ^ CORE]
    for n in range(count):
        hold(n).wait()


def in_vmem(value):
    return pltpu.with_memory_space_constraint(value, pltpu.VMEM)


def in_hbm(value):
    return pltpu.with_memory_space_constraint(value, pltpu.HBM)


WHOLE = pl.BlockSpec(memory_space=pltpu.VMEM)
SCALARS = pl.BlockSpec(memory_space=pltpu.SMEM)


def turn(hidden, out_grad, place):
    tokens, width = hidden.shape
    rows = width // SHARDS
    step = min(256, tokens)
    steps = tokens // step
    shape = pltpu.VMEM((2, 2, 2, rows, tokens), BF)
    far = pl.BlockSpec(memory_space=pltpu.HBM)
    return pl.pallas_call(
        turn_kernel,
        in_specs=[SCALARS, far, far],
        out_specs=[WHOLE] * 3,
        scratch_shapes=[
            pltpu.VMEM((steps, step, width), BF),
            pltpu.VMEM((SHARDS, rows, step), BF),
            pltpu.SemaphoreType.DMA((steps,)),
            pltpu.SemaphoreType.DMA((steps,)),
        ],
        out_shape=[shape, shape, pltpu.VMEM((tokens, CHUNKS[0][1]), BF)],
        compiler_params=params(),
        cost_estimate=LIGHT,
        name="turn",
    )(place, in_hbm(hidden), in_hbm(out_grad))


def product_kernel(added, following, spot, turned, step, place, left_ref, right_ref, *refs):
    depth = left_ref.shape[-1]
    out_ref = refs[added + int(following is not None)]
    if following is not None:
        grad_ref, next_ref, sem = refs[added], refs[added + 2], refs[added + 3]
        ahead = pltpu.make_async_copy(grad_ref.at[:, pl.ds(following, next_ref.shape[1])], next_ref, sem)
        ahead.start()
    left = left_ref[spot].reshape(-1, depth)
    flat = len(out_ref.shape) - 1

    def columns(t, _):
        here = pl.ds(pl.multiple_of(t * step, 128), step)
        total = jnp.dot(left, right_ref[:, here], preferred_element_type=F32)
        total = total.reshape(*out_ref.shape[:-1], step)
        for n in range(added):
            total += refs[n][(*spot, slice(None), here)].astype(F32)
        total = total.astype(BF)
        if turned:
            for p in range(2):
                for q in range(2):
                    out_ref[q, p, :, here] = total[p, q]
        else:
            out_ref[(*(slice(None),) * flat, here)] = total
        return 0

    lax.fori_loop(0, out_ref.shape[-1] // step, columns, 0)
    if following is not None:
        ahead.wait()


def product(place, left, right, order=None, bit=0, add=None, grad=None, following=None):
    rows = left.shape[3]
    depth, width = right.shape
    dim = order[0] if order else None
    turned = bool(order) and order[1] > order[2]
    spot = tuple(bit if d == dim else slice(None) for d in range(3))
    kept = (2,) * (3 if dim is None else 2)
    args = [left, right] + ([] if add is None else [add])
    specs = [WHOLE] * len(args)
    args = [in_vmem(a) for a in args]
    outs = [pltpu.VMEM((*kept, rows, width), BF)]
    scratch = []
    if following is not None:
        column, follow_width, _ = CHUNKS[following]
        specs.append(pl.BlockSpec(memory_space=pltpu.HBM))
        args.append(in_hbm(grad))
        outs.append(pltpu.VMEM((depth, follow_width), BF))
        scratch.append(pltpu.SemaphoreType.DMA(()))
    else:
        column = None
    return pl.pallas_call(
        functools.partial(product_kernel, int(add is not None), column, spot, turned, width // 2),
        in_specs=[SCALARS] + specs,
        out_specs=[WHOLE] * len(outs),
        out_shape=outs,
        scratch_shapes=scratch,
        compiler_params=params(),
        cost_estimate=LIGHT,
        name="product",
    )(place, *args)


def adam_kernel(chained, column, group_column, place, *refs):
    mine_ref, came_ref, first_ref, second_ref, param_ref, anchor_ref, moment_ref = refs[:7]
    first_out, second_out = refs[7 + chained : 9 + chained]
    parts = refs[9 + chained : 13 + chained]
    quarters = refs[13 + chained]
    step = quarters.shape[-1]

    def columns(t, _):
        near = pl.ds(pl.multiple_of(t * step, 128), step)
        here = pl.ds(pl.multiple_of(column + t * step, 128), step)
        gradient = mine_ref[:, near].astype(F32) + came_ref[:, near].astype(F32)
        first_fresh = beta_first * first_ref[0, :, here].astype(F32) + (1.0 - beta_first) * gradient
        second_fresh = beta_second * second_ref[0, :, here].astype(F32) + (1.0 - beta_second) * gradient * gradient
        level = second_fresh * (1.0 / bias_second)
        root = level * lax.rsqrt(level)
        stepped = (1.0 - inner_rate * decay_rate) * param_ref[0, :, here]
        stepped = stepped - first_fresh * (inner_rate / bias_first) / (root + epsilon)
        first_out[0, :, here] = first_fresh.astype(BF)
        second_out[0, :, here] = second_fresh.astype(BF)
        departure = (anchor_ref[:, here] - stepped) * (pseudo_weight / REPLICAS) + moment_ref[:, here]
        quarters[...] = departure.reshape(quarters.shape)
        wide = pl.ds(pl.multiple_of(group_column + t * step, 128), step)
        for distance in range(4):
            parts[distance][:, wide] = quarters[place[1] ^ distance].astype(BF)
        return 0

    lax.fori_loop(0, mine_ref.shape[-1] // step, columns, 0)


def adam(place, grads, first, second, param, anchor, moment, column, width, before, group_column, group_width):
    rows, total_width = anchor.shape
    part = rows // 4
    part_shape = pltpu.VMEM((part, group_width), BF)
    firsts, seconds, parts = before
    chain = [(0, firsts), (1, seconds)] + [(2 + d, p) for d, p in enumerate(parts or ())]
    chain = [(o, a) for o, a in chain if a is not None]
    outs = pl.pallas_call(
        functools.partial(adam_kernel, len(chain), column, group_column),
        in_specs=[SCALARS] + [WHOLE] * (7 + len(chain)),
        out_specs=[WHOLE] * 6,
        scratch_shapes=[pltpu.VMEM((4, part, 128), F32)],
        out_shape=[pltpu.VMEM(first.shape, BF)] * 2 + [part_shape] * 4,
        input_output_aliases={8 + n: o for n, (o, _) in enumerate(chain)},
        compiler_params=params(),
        cost_estimate=LIGHT,
        name="adam",
    )(place, *(in_vmem(a) for a in (*grads, first, second, param, anchor, moment)), *(in_vmem(a) for _, a in chain))
    return outs[0], outs[1], outs[2:]


def hold_kernel(place, first, second, param, anchor, moment, *refs):
    outs, sems = refs[:5], refs[6]
    share_ref = refs[5]
    copies = [
        pltpu.make_async_copy(source, target, sems.at[n])
        for n, (source, target) in enumerate(zip((first, second, param, anchor, moment), (*outs[:4], share_ref)))
    ]
    for copy in copies:
        copy.start()
    placed = outs[4]
    width = share_ref.shape[1]
    placed[...] = jnp.zeros_like(placed)
    copies[4].wait()
    placed[:, pl.ds(pl.multiple_of(place[2] * width, 128), width)] = moment_weight * share_ref[...]
    for copy in copies[:4]:
        copy.wait()


def hold(place, first, second, param, anchor, moment):
    far = pl.BlockSpec(memory_space=pltpu.HBM)
    args = (first, second, param, anchor, moment)
    return pl.pallas_call(
        hold_kernel,
        in_specs=[SCALARS] + [far] * 5,
        out_specs=[WHOLE] * 5,
        out_shape=[pltpu.VMEM(a.shape, a.dtype) for a in args[:4]] + [pltpu.VMEM(anchor.shape, F32)],
        scratch_shapes=[pltpu.VMEM(moment.shape, F32), pltpu.SemaphoreType.DMA((5,))],
        compiler_params=params(),
        cost_estimate=LIGHT,
        name="hold",
    )(place, *(in_hbm(a) for a in args))


def store_kernel(place, first, second, part, first_out, second_out, part_out, sems):
    copies = [
        pltpu.make_async_copy(source, target, sems.at[n])
        for n, (source, target) in enumerate(((first, first_out), (second, second_out)))
    ]
    for copy in copies:
        copy.start()
    for copy in copies:
        copy.wait()


def store(place, first, second, part):
    far = pl.BlockSpec(memory_space=pltpu.HBM)
    return pl.pallas_call(
        store_kernel,
        in_specs=[SCALARS, WHOLE, WHOLE, WHOLE],
        out_specs=[far, far, WHOLE],
        out_shape=[pltpu.HBM(first.shape, BF)] * 2 + [pltpu.VMEM(part.shape, part.dtype)],
        scratch_shapes=[pltpu.SemaphoreType.DMA((2,))],
        input_output_aliases={3: 2},
        compiler_params=params(),
        cost_estimate=LIGHT,
        name="store",
    )(place, in_vmem(first), in_vmem(second), in_vmem(part))


def last_kernel(chained, final, column, place, p0, p1, p2, p3, anchor_ref, moment_ref, *refs):
    refs = refs[chained:]
    params_out, total_out = refs[:2]
    fresh, quarters, sems = refs[-3:]
    step = quarters.shape[-1]

    def columns(t, _):
        near = pl.ds(pl.multiple_of(t * step, 128), step)
        here = pl.ds(pl.multiple_of(column + t * step, 128), step)
        for distance, piece in enumerate((p0, p1, p2, p3)):
            quarters[place[1] ^ distance] = piece[:, near].astype(F32)
        total = quarters[...].reshape(-1, step)
        fresh[:, near] = anchor_ref[:, here] - outer_rate * total
        total_out[:, here] = total
        return 0

    lax.fori_loop(0, fresh.shape[-1] // step, columns, 0)
    copies = [pltpu.make_async_copy(fresh, params_out.at[:, pl.ds(column, fresh.shape[-1])], sems.at[0])]
    copies[0].start()
    if final:
        moment_out, moment = refs[2:4]
        width = moment.shape[-1]
        share = pl.ds(pl.multiple_of(place[2] * width, 128), width)
        weighted = moment_ref[:, share]
        pseudo = (total_out[:, share] - weighted) * (1.0 / pseudo_weight)
        moment[...] = weighted * (outer_beta / moment_weight) + pseudo
        copies.append(pltpu.make_async_copy(moment, moment_out, sems.at[1]))
        copies[1].start()
    for copy in copies:
        copy.wait()


def last(place, pieces, anchor, moment, column, width, before, share):
    rows = anchor.shape[0]
    chain = [a for a in before if a is not None]
    if chain:
        chain = [in_hbm(chain[0]), in_vmem(chain[1])]
    far = pl.BlockSpec(memory_space=pltpu.HBM)
    final = share is not None
    return pl.pallas_call(
        functools.partial(last_kernel, len(chain), final, column),
        in_specs=[SCALARS] + [WHOLE] * 6 + [far, WHOLE][: len(chain)],
        out_specs=[far, WHOLE] + [far] * final,
        out_shape=[pltpu.HBM(anchor.shape, F32), pltpu.VMEM(anchor.shape, F32)]
        + ([pltpu.HBM((rows, share), F32)] if final else []),
        scratch_shapes=([pltpu.VMEM((rows, share), F32)] if final else [])
        + [
            pltpu.VMEM((rows, width), F32),
            pltpu.VMEM((4, rows // 4, 128), F32),
            pltpu.SemaphoreType.DMA((2,)),
        ],
        input_output_aliases={7 + n: n for n in range(len(chain))},
        compiler_params=params(),
        cost_estimate=LIGHT,
        name="last",
    )(place, *(in_vmem(a) for a in (*pieces, anchor, moment)), *chain)


def add(*values):
    total = values[0].astype(F32)
    for value in values[1:]:
        total = total + value.astype(F32)
    return total.astype(BF)


def body(hidden, out_grad, inner_params, first_moment, second_moment, anchor, outer_moment):
    me = lax.axis_index("shard")
    rep = lax.axis_index("rep")
    place = jnp.stack([me, rep % 4, rep]).astype(jnp.int32)
    own, other, held = turn(hidden, out_grad, place)
    held = [held]
    count = len(CHUNKS)
    across, kept, arrived, twice, thrice = ([None] * count for _ in range(5))
    group_of = {n: g for g, group in enumerate(GROUPS) for n in group}
    parts, sums = [None] * len(GROUPS), [None] * len(GROUPS)
    firsts = seconds = None
    result = [None, None]
    token = place

    for kind, n in PLAN:
        column, width, order = CHUNKS[n]
        if kind == "other":
            following = n + 1 if n + 1 < count else None
            done, *more = product(token, other, held[n], grad=out_grad, following=following)
            held += more
            across[n] = swap(done, CORE)
        elif kind == "send":
            (done,) = product(token, own, held[n], order, 1, across[n])
            arrived[n] = swap(done, MASKS[order[0]])
        elif kind == "keep":
            (done,) = product(token, own, held[n], order, 0, across[n])
            kept[n] = done
        elif kind == "hold":
            first_held, second_held, param_held, anchor_held, moment_held = hold(
                token, first_moment, second_moment, inner_params, anchor, outer_moment
            )
            done = moment_held
        elif kind == "fold":
            mine, token = lax.optimization_barrier((kept[n], token))
            done = add(mine[1], arrived[n][1])
            twice[n] = (add(mine[0], arrived[n][0]), swap(done, MASKS[order[1]]))
        elif kind == "again":
            came = twice[n][1]
            mine, token = lax.optimization_barrier((twice[n][0], token))
            done = add(mine[1], came[1])
            thrice[n] = (add(mine[0], came[0]), swap(done, MASKS[order[2]]))
        elif kind == "adam":
            group = group_of[n]
            group_column = CHUNKS[GROUPS[group][0]][0]
            group_width = sum(CHUNKS[m][1] for m in GROUPS[group])
            firsts, seconds, parts[group] = adam(
                token, thrice[n], first_held, second_held, param_held, anchor_held, moment_held,
                column, width, (firsts, seconds, parts[group]), column - group_column, group_width,
            )
            done = parts[group][0]
            if n == GROUPS[group][-1]:
                parts[group] = [done] + [swap_rep(parts[group][d], d) for d in (1, 2, 3)]
        elif kind == "store":
            firsts, seconds, done = store(token, firsts, seconds, parts[n][0])
            parts[n][0] = done
        elif kind == "sum":
            mine, token = lax.optimization_barrier((parts[n][0], token))
            done = add(mine, *parts[n][1:])
            sums[n] = (done, swap_rep(done, 4))
        elif kind == "total":
            mine, token = lax.optimization_barrier((sums[n][0], token))
            done = add(mine, sums[n][1])
            sums[n] = [done] + [swap_rep(done, d) for d in (1, 2, 3)]
        elif kind == "last":
            column = CHUNKS[GROUPS[n][0]][0]
            width = sum(CHUNKS[m][1] for m in GROUPS[n])
            share = outer_moment.shape[1] if n == len(GROUPS) - 1 else None
            result = last(token, sums[n], anchor_held, moment_held, column, width, result, share)
            done = result[1]
        token, _ = lax.optimization_barrier((token, done))
    params_new, _, moment_new = result
    return (params_new, firsts, seconds, moment_new)


def solution(mesh):
    placed = (
        P(("rep", "shard"), None),
        P(("rep", "shard"), None),
        P("rep", "shard", None),
        P("rep", "shard", None),
        P("rep", "shard", None),
        P("shard", None),
        P("shard", "rep"),
    )
    return jax.shard_map(
        body,
        mesh=mesh,
        in_specs=placed,
        out_specs=(
            P("shard", None),
            P("rep", "shard", None),
            P("rep", "shard", None),
            P("shard", "rep"),
        ),
        check_vma=False,
    )
```

```python
import functools

import jax
import jax.numpy as jnp
from jax import lax
from jax.experimental import pallas as pl
from jax.experimental.pallas import tpu as pltpu
from jax.sharding import PartitionSpec as P

beta_first = 0.9
beta_second = 0.95
bias_first = 1.0 - 0.9**30
bias_second = 1.0 - 0.95**30
inner_rate = 0.05
decay_rate = 0.1
epsilon = 1e-08
outer_beta = 0.9
outer_rate = 0.7

pseudo_weight = 1.0 + outer_beta
moment_weight = outer_beta * outer_beta

SHARDS = 16
REPLICAS = 8
BF = jnp.bfloat16
F32 = jnp.float32
LIMIT = 20 * 1024 * 1024
LIGHT = pl.CostEstimate(flops=0, bytes_accessed=1024, transcendentals=0)

CORE = 1
MASKS = (2, 4, 12)
Z_ORDER = (2, 1, 3)
CHUNKS = (
    (0, 1792, (2, 0, 1)),
    (1792, 1792, (0, 1, 2)),
    (3584, 1536, (1, 2, 0)),
)
GROUPS = ((0, 1), (2,))
PLAN = (
    *(("other", n) for n in range(3)),
    *(("send", n) for n in range(3)),
    *(("keep", n) for n in range(3)),
    ("hold", 0),
    *(("fold", n) for n in range(3)),
    *(("again", n) for n in range(3)),
    *(("adam", n) for n in range(3)),
    ("store", 0),
    *((kind, n) for kind in ("sum", "total", "last") for n in range(2)),
)


def swap(value, mask):
    return lax.ppermute(value, "shard", [(i, i ^ mask) for i in range(SHARDS)])


def swap_rep(value, mask):
    return lax.ppermute(value, "rep", [(i, i ^ mask) for i in range(REPLICAS)])


def spread(values):
    got = {d: swap_rep(values[d - 1], d) for d in Z_ORDER}
    return [got[d] for d in (1, 2, 3)]


def params(**kw):
    return pltpu.CompilerParams(vmem_limit_bytes=LIMIT, **kw)


def turn_kernel(place, hidden_ref, grad_ref, own_ref, other_ref, held_ref, landed, turned, sems, grad_sems):
    count, step, _ = landed.shape
    strip = grad_ref.shape[0] // count

    def fetch(n):
        return pltpu.make_async_copy(hidden_ref.at[pl.ds(n * step, step)], landed.at[n], sems.at[n])

    def hold(n):
        rows = pl.ds(n * strip, strip)
        return pltpu.make_async_copy(grad_ref.at[rows, pl.ds(0, held_ref.shape[1])], held_ref.at[rows], grad_sems.at[n])

    for n in range(count):
        fetch(n).start()
    for n in range(count):
        hold(n).start()
    me = place[0]
    for n in range(count):
        fetch(n).wait()
        turned[...] = landed[n].T.reshape(turned.shape)
        tokens = slice(n * step, (n + 1) * step)
        for bx in range(2):
            for ba in range(2):
                for bb in range(2):
                    mask = (bx * MASKS[0]) ^ (ba * MASKS[1]) ^ (bb * MASKS[2])
                    own_ref[bx, ba, bb, :, tokens] = turned[me ^ mask]
                    other_ref[bx, ba, bb, :, tokens] = turned[me ^ mask ^ CORE]
    for n in range(count):
        hold(n).wait()


def in_vmem(value):
    return pltpu.with_memory_space_constraint(value, pltpu.VMEM)


def in_hbm(value):
    return pltpu.with_memory_space_constraint(value, pltpu.HBM)


WHOLE = pl.BlockSpec(memory_space=pltpu.VMEM)
SCALARS = pl.BlockSpec(memory_space=pltpu.SMEM)


def turn(hidden, out_grad, place):
    tokens, width = hidden.shape
    rows = width // SHARDS
    step = min(256, tokens)
    steps = tokens // step
    shape = pltpu.VMEM((2, 2, 2, rows, tokens), BF)
    far = pl.BlockSpec(memory_space=pltpu.HBM)
    return pl.pallas_call(
        turn_kernel,
        in_specs=[SCALARS, far, far],
        out_specs=[WHOLE] * 3,
        scratch_shapes=[
            pltpu.VMEM((steps, step, width), BF),
            pltpu.VMEM((SHARDS, rows, step), BF),
            pltpu.SemaphoreType.DMA((steps,)),
            pltpu.SemaphoreType.DMA((steps,)),
        ],
        out_shape=[shape, shape, pltpu.VMEM((tokens, CHUNKS[0][1]), BF)],
        compiler_params=params(),
        cost_estimate=LIGHT,
        name="turn",
    )(place, in_hbm(hidden), in_hbm(out_grad))


def product_kernel(added, following, spot, turned, step, place, left_ref, right_ref, *refs):
    depth = left_ref.shape[-1]
    out_ref = refs[added + int(following is not None)]
    if following is not None:
        grad_ref, next_ref, sem = refs[added], refs[added + 2], refs[added + 3]
        ahead = pltpu.make_async_copy(grad_ref.at[:, pl.ds(following, next_ref.shape[1])], next_ref, sem)
        ahead.start()
    flat = len(out_ref.shape) - 1

    def columns(t, _):
        here = pl.ds(pl.multiple_of(t * step, 128), step)
        left = left_ref[spot].reshape(-1, depth)
        total = jnp.dot(left, right_ref[:, here], preferred_element_type=F32)
        total = total.reshape(*out_ref.shape[:-1], step)
        for n in range(added):
            total += refs[n][(*spot, slice(None), here)].astype(F32)
        total = total.astype(BF)
        if turned:
            for p in range(2):
                for q in range(2):
                    out_ref[q, p, :, here] = total[p, q]
        else:
            out_ref[(*(slice(None),) * flat, here)] = total
        return 0

    lax.fori_loop(0, out_ref.shape[-1] // step, columns, 0)
    if following is not None:
        ahead.wait()


def product(place, left, right, order=None, bit=0, add=None, grad=None, following=None):
    rows = left.shape[3]
    depth, width = right.shape
    dim = order[0] if order else None
    turned = bool(order) and order[1] > order[2]
    spot = tuple(bit if d == dim else slice(None) for d in range(3))
    kept = (2,) * (3 if dim is None else 2)
    args = [left, right] + ([] if add is None else [add])
    specs = [WHOLE] * len(args)
    args = [in_vmem(a) for a in args]
    outs = [pltpu.VMEM((*kept, rows, width), BF)]
    scratch = []
    if following is not None:
        column, follow_width, _ = CHUNKS[following]
        specs.append(pl.BlockSpec(memory_space=pltpu.HBM))
        args.append(in_hbm(grad))
        outs.append(pltpu.VMEM((depth, follow_width), BF))
        scratch.append(pltpu.SemaphoreType.DMA(()))
    else:
        column = None
    return pl.pallas_call(
        functools.partial(product_kernel, int(add is not None), column, spot, turned, width // 2),
        in_specs=[SCALARS] + specs,
        out_specs=[WHOLE] * len(outs),
        out_shape=outs,
        scratch_shapes=scratch,
        compiler_params=params(),
        cost_estimate=LIGHT,
        name="product",
    )(place, *args)


def adam_kernel(chained, column, group_column, place, *refs):
    mine_ref, came_ref, first_ref, second_ref, param_ref, anchor_ref, moment_ref = refs[:7]
    first_out, second_out = refs[7 + chained : 9 + chained]
    parts = refs[9 + chained : 13 + chained]
    quarters = refs[13 + chained]
    step = quarters.shape[-1]

    def columns(t, _):
        near = pl.ds(pl.multiple_of(t * step, 128), step)
        here = pl.ds(pl.multiple_of(column + t * step, 128), step)
        gradient = mine_ref[:, near].astype(F32) + came_ref[:, near].astype(F32)
        first_fresh = beta_first * first_ref[0, :, here].astype(F32) + (1.0 - beta_first) * gradient
        second_fresh = beta_second * second_ref[0, :, here].astype(F32) + (1.0 - beta_second) * gradient * gradient
        level = second_fresh * (1.0 / bias_second)
        root = level * lax.rsqrt(level)
        stepped = (1.0 - inner_rate * decay_rate) * param_ref[0, :, here]
        stepped = stepped - first_fresh * (inner_rate / bias_first) / (root + epsilon)
        first_out[0, :, here] = first_fresh.astype(BF)
        second_out[0, :, here] = second_fresh.astype(BF)
        departure = (anchor_ref[:, here] - stepped) * (pseudo_weight / REPLICAS) + moment_ref[:, here]
        quarters[...] = departure.reshape(quarters.shape)
        wide = pl.ds(pl.multiple_of(group_column + t * step, 128), step)
        for distance in range(4):
            parts[distance][:, wide] = quarters[place[1] ^ distance].astype(BF)
        return 0

    lax.fori_loop(0, mine_ref.shape[-1] // step, columns, 0)


def adam(place, grads, first, second, param, anchor, moment, column, width, before, group_column, group_width):
    rows, total_width = anchor.shape
    part = rows // 4
    part_shape = pltpu.VMEM((part, group_width), BF)
    firsts, seconds, parts = before
    chain = [(0, firsts), (1, seconds)] + [(2 + d, p) for d, p in enumerate(parts or ())]
    chain = [(o, a) for o, a in chain if a is not None]
    outs = pl.pallas_call(
        functools.partial(adam_kernel, len(chain), column, group_column),
        in_specs=[SCALARS] + [WHOLE] * (7 + len(chain)),
        out_specs=[WHOLE] * 6,
        scratch_shapes=[pltpu.VMEM((4, part, 128), F32)],
        out_shape=[pltpu.VMEM(first.shape, BF)] * 2 + [part_shape] * 4,
        input_output_aliases={8 + n: o for n, (o, _) in enumerate(chain)},
        compiler_params=params(),
        cost_estimate=LIGHT,
        name="adam",
    )(place, *(in_vmem(a) for a in (*grads, first, second, param, anchor, moment)), *(in_vmem(a) for _, a in chain))
    return outs[0], outs[1], outs[2:]


def hold_kernel(place, first, second, param, anchor, moment, *refs):
    outs, sems = refs[:5], refs[6]
    share_ref = refs[5]
    copies = [
        pltpu.make_async_copy(source, target, sems.at[n])
        for n, (source, target) in enumerate(zip((first, second, param, anchor, moment), (*outs[:4], share_ref)))
    ]
    for copy in copies:
        copy.start()
    placed = outs[4]
    width = share_ref.shape[1]
    placed[...] = jnp.zeros_like(placed)
    copies[4].wait()
    placed[:, pl.ds(pl.multiple_of(place[2] * width, 128), width)] = moment_weight * share_ref[...]
    for copy in copies[:4]:
        copy.wait()


def hold(place, first, second, param, anchor, moment):
    far = pl.BlockSpec(memory_space=pltpu.HBM)
    args = (first, second, param, anchor, moment)
    return pl.pallas_call(
        hold_kernel,
        in_specs=[SCALARS] + [far] * 5,
        out_specs=[WHOLE] * 5,
        out_shape=[pltpu.VMEM(a.shape, a.dtype) for a in args[:4]] + [pltpu.VMEM(anchor.shape, F32)],
        scratch_shapes=[pltpu.VMEM(moment.shape, F32), pltpu.SemaphoreType.DMA((5,))],
        compiler_params=params(),
        cost_estimate=LIGHT,
        name="hold",
    )(place, *(in_hbm(a) for a in args))


def store_kernel(place, first, second, part, first_out, second_out, part_out, sems):
    copies = [
        pltpu.make_async_copy(source, target, sems.at[n])
        for n, (source, target) in enumerate(((first, first_out), (second, second_out)))
    ]
    for copy in copies:
        copy.start()
    for copy in copies:
        copy.wait()


def store(place, first, second, part):
    far = pl.BlockSpec(memory_space=pltpu.HBM)
    return pl.pallas_call(
        store_kernel,
        in_specs=[SCALARS, WHOLE, WHOLE, WHOLE],
        out_specs=[far, far, WHOLE],
        out_shape=[pltpu.HBM(first.shape, BF)] * 2 + [pltpu.VMEM(part.shape, part.dtype)],
        scratch_shapes=[pltpu.SemaphoreType.DMA((2,))],
        input_output_aliases={3: 2},
        compiler_params=params(),
        cost_estimate=LIGHT,
        name="store",
    )(place, in_vmem(first), in_vmem(second), in_vmem(part))


def last_kernel(chained, final, column, place, p0, p1, p2, p3, anchor_ref, moment_ref, *refs):
    refs = refs[chained:]
    params_out, total_out = refs[:2]
    fresh, quarters, sems = refs[-3:]
    step = quarters.shape[-1]

    def columns(t, _):
        near = pl.ds(pl.multiple_of(t * step, 128), step)
        here = pl.ds(pl.multiple_of(column + t * step, 128), step)
        for distance, piece in enumerate((p0, p1, p2, p3)):
            quarters[place[1] ^ distance] = piece[:, near].astype(F32)
        total = quarters[...].reshape(-1, step)
        fresh[:, near] = anchor_ref[:, here] - outer_rate * total
        total_out[:, here] = total
        return 0

    copies = []
    tiles = fresh.shape[-1] // step
    for n, (begin, end) in enumerate(((0, tiles // 2), (tiles // 2, tiles))):
        lax.fori_loop(begin, end, columns, 0)
        wide = (end - begin) * step
        copy = pltpu.make_async_copy(
            fresh.at[:, pl.ds(begin * step, wide)], params_out.at[:, pl.ds(column + begin * step, wide)], sems.at[n]
        )
        copy.start()
        copies.append(copy)
    if final:
        moment_out, moment = refs[2:4]
        width = moment.shape[-1]
        share = pl.ds(pl.multiple_of(place[2] * width, 128), width)
        weighted = moment_ref[:, share]
        pseudo = (total_out[:, share] - weighted) * (1.0 / pseudo_weight)
        moment[...] = weighted * (outer_beta / moment_weight) + pseudo
        copies.append(pltpu.make_async_copy(moment, moment_out, sems.at[2]))
        copies[2].start()
    for copy in copies:
        copy.wait()


def last(place, pieces, anchor, moment, column, width, before, share):
    rows = anchor.shape[0]
    chain = [a for a in before if a is not None]
    if chain:
        chain = [in_hbm(chain[0]), in_vmem(chain[1])]
    far = pl.BlockSpec(memory_space=pltpu.HBM)
    final = share is not None
    return pl.pallas_call(
        functools.partial(last_kernel, len(chain), final, column),
        in_specs=[SCALARS] + [WHOLE] * 6 + [far, WHOLE][: len(chain)],
        out_specs=[far, WHOLE] + [far] * final,
        out_shape=[pltpu.HBM(anchor.shape, F32), pltpu.VMEM(anchor.shape, F32)]
        + ([pltpu.HBM((rows, share), F32)] if final else []),
        scratch_shapes=([pltpu.VMEM((rows, share), F32)] if final else [])
        + [
            pltpu.VMEM((rows, width), F32),
            pltpu.VMEM((4, rows // 4, 128), F32),
            pltpu.SemaphoreType.DMA((3,)),
        ],
        input_output_aliases={7 + n: n for n in range(len(chain))},
        compiler_params=params(),
        cost_estimate=LIGHT,
        name="last",
    )(place, *(in_vmem(a) for a in (*pieces, anchor, moment)), *chain)


def add(*values):
    total = values[0].astype(F32)
    for value in values[1:]:
        total = total + value.astype(F32)
    return total.astype(BF)


def body(hidden, out_grad, inner_params, first_moment, second_moment, anchor, outer_moment):
    me = lax.axis_index("shard")
    rep = lax.axis_index("rep")
    place = jnp.stack([me, rep % 4, rep]).astype(jnp.int32)
    own, other, held = turn(hidden, out_grad, place)
    held = [held]
    count = len(CHUNKS)
    across, kept, arrived, twice, thrice = ([None] * count for _ in range(5))
    group_of = {n: g for g, group in enumerate(GROUPS) for n in group}
    parts, sums = [None] * len(GROUPS), [None] * len(GROUPS)
    firsts = seconds = None
    result = [None, None]
    token = place

    for kind, n in PLAN:
        column, width, order = CHUNKS[n]
        if kind == "other":
            following = n + 1 if n + 1 < count else None
            done, *more = product(token, other, held[n], grad=out_grad, following=following)
            held += more
            across[n] = swap(done, CORE)
        elif kind == "send":
            (done,) = product(token, own, held[n], order, 1, across[n])
            arrived[n] = swap(done, MASKS[order[0]])
        elif kind == "keep":
            (done,) = product(token, own, held[n], order, 0, across[n])
            kept[n] = done
        elif kind == "hold":
            first_held, second_held, param_held, anchor_held, moment_held = hold(
                token, first_moment, second_moment, inner_params, anchor, outer_moment
            )
            done = moment_held
        elif kind == "fold":
            mine, token = lax.optimization_barrier((kept[n], token))
            done = add(mine[1], arrived[n][1])
            twice[n] = (add(mine[0], arrived[n][0]), swap(done, MASKS[order[1]]))
        elif kind == "again":
            came = twice[n][1]
            mine, token = lax.optimization_barrier((twice[n][0], token))
            done = add(mine[1], came[1])
            thrice[n] = (add(mine[0], came[0]), swap(done, MASKS[order[2]]))
        elif kind == "adam":
            group = group_of[n]
            group_column = CHUNKS[GROUPS[group][0]][0]
            group_width = sum(CHUNKS[m][1] for m in GROUPS[group])
            firsts, seconds, parts[group] = adam(
                token, thrice[n], first_held, second_held, param_held, anchor_held, moment_held,
                column, width, (firsts, seconds, parts[group]), column - group_column, group_width,
            )
            done = parts[group][0]
            if n == GROUPS[group][-1]:
                parts[group] = [done] + spread([parts[group][d] for d in (1, 2, 3)])
        elif kind == "store":
            firsts, seconds, done = store(token, firsts, seconds, parts[n][0])
            parts[n][0] = done
        elif kind == "sum":
            mine, token = lax.optimization_barrier((parts[n][0], token))
            done = add(mine, *parts[n][1:])
            sums[n] = (done, swap_rep(done, 4))
        elif kind == "total":
            mine, token = lax.optimization_barrier((sums[n][0], token))
            done = add(mine, sums[n][1])
            sums[n] = [done] + spread([done] * 3)
        elif kind == "last":
            column = CHUNKS[GROUPS[n][0]][0]
            width = sum(CHUNKS[m][1] for m in GROUPS[n])
            share = outer_moment.shape[1] if n == len(GROUPS) - 1 else None
            result = last(token, sums[n], anchor_held, moment_held, column, width, result, share)
            done = result[1]
        token, _ = lax.optimization_barrier((token, done))
    params_new, _, moment_new = result
    return (params_new, firsts, seconds, moment_new)


def solution(mesh):
    placed = (
        P(("rep", "shard"), None),
        P(("rep", "shard"), None),
        P("rep", "shard", None),
        P("rep", "shard", None),
        P("rep", "shard", None),
        P("shard", None),
        P("shard", "rep"),
    )
    return jax.shard_map(
        body,
        mesh=mesh,
        in_specs=placed,
        out_specs=(
            P("shard", None),
            P("rep", "shard", None),
            P("rep", "shard", None),
            P("shard", "rep"),
        ),
        check_vma=False,
    )
```

```python
import functools

import jax
import jax.numpy as jnp
from jax import lax
from jax.experimental import pallas as pl
from jax.experimental.pallas import tpu as pltpu
from jax.sharding import PartitionSpec as P

beta_first = 0.9
beta_second = 0.95
bias_first = 1.0 - 0.9**30
bias_second = 1.0 - 0.95**30
inner_rate = 0.05
decay_rate = 0.1
epsilon = 1e-08
outer_beta = 0.9
outer_rate = 0.7

pseudo_weight = 1.0 + outer_beta
moment_weight = outer_beta * outer_beta

SHARDS = 16
REPLICAS = 8
BF = jnp.bfloat16
F32 = jnp.float32
LIMIT = 20 * 1024 * 1024
LIGHT = pl.CostEstimate(flops=0, bytes_accessed=1024, transcendentals=0)

CORE = 1
MASKS = (2, 4, 12)
CHUNKS = (
    (0, 1792, (0, 1, 2)),
    (1792, 1792, (1, 2, 0)),
    (3584, 1536, (2, 0, 1)),
)
GROUPS = ((0, 1), (2,))
PLAN = (
    *(("other", n) for n in range(3)),
    *(("send", n) for n in range(3)),
    *(("keep", n) for n in range(3)),
    *(("fold", n) for n in range(3)),
    ("hold", 0),
    *(("again", n) for n in range(3)),
    *(("adam", n) for n in range(3)),
    ("store", 0),
    *((kind, n) for kind in ("sum", "total", "last") for n in range(2)),
)


def swap(value, mask):
    return lax.ppermute(value, "shard", [(i, i ^ mask) for i in range(SHARDS)])


def swap_rep(value, mask):
    return lax.ppermute(value, "rep", [(i, i ^ mask) for i in range(REPLICAS)])


def params(**kw):
    return pltpu.CompilerParams(vmem_limit_bytes=LIMIT, **kw)


def turn_kernel(place, hidden_ref, grad_ref, own_ref, other_ref, held_ref, landed, turned, sems, grad_sems):
    count, step, _ = landed.shape
    strip = grad_ref.shape[0] // count

    def fetch(n):
        return pltpu.make_async_copy(hidden_ref.at[pl.ds(n * step, step)], landed.at[n], sems.at[n])

    def hold(n):
        rows = pl.ds(n * strip, strip)
        return pltpu.make_async_copy(grad_ref.at[rows, pl.ds(0, held_ref.shape[1])], held_ref.at[rows], grad_sems.at[n])

    for n in range(count):
        fetch(n).start()
    for n in range(count):
        hold(n).start()
    me = place[0]
    for n in range(count):
        fetch(n).wait()
        turned[...] = landed[n].T.reshape(turned.shape)
        tokens = slice(n * step, (n + 1) * step)
        for bx in range(2):
            for ba in range(2):
                for bb in range(2):
                    mask = (bx * MASKS[0]) ^ (ba * MASKS[1]) ^ (bb * MASKS[2])
                    own_ref[bx, ba, bb, :, tokens] = turned[me ^ mask]
                    other_ref[bx, ba, bb, :, tokens] = turned[me ^ mask ^ CORE]
    for n in range(count):
        hold(n).wait()


def in_vmem(value):
    return pltpu.with_memory_space_constraint(value, pltpu.VMEM)


def in_hbm(value):
    return pltpu.with_memory_space_constraint(value, pltpu.HBM)


WHOLE = pl.BlockSpec(memory_space=pltpu.VMEM)
SCALARS = pl.BlockSpec(memory_space=pltpu.SMEM)


def turn(hidden, out_grad, place):
    tokens, width = hidden.shape
    rows = width // SHARDS
    step = min(256, tokens)
    steps = tokens // step
    shape = pltpu.VMEM((2, 2, 2, rows, tokens), BF)
    far = pl.BlockSpec(memory_space=pltpu.HBM)
    return pl.pallas_call(
        turn_kernel,
        in_specs=[SCALARS, far, far],
        out_specs=[WHOLE] * 3,
        scratch_shapes=[
            pltpu.VMEM((steps, step, width), BF),
            pltpu.VMEM((SHARDS, rows, step), BF),
            pltpu.SemaphoreType.DMA((steps,)),
            pltpu.SemaphoreType.DMA((steps,)),
        ],
        out_shape=[shape, shape, pltpu.VMEM((tokens, CHUNKS[0][1]), BF)],
        compiler_params=params(),
        cost_estimate=LIGHT,
        name="turn",
    )(place, in_hbm(hidden), in_hbm(out_grad))


def product_kernel(added, following, spot, turned, step, place, left_ref, right_ref, *refs):
    depth = left_ref.shape[-1]
    out_ref = refs[added + int(following is not None)]
    if following is not None:
        grad_ref, next_ref, sem = refs[added], refs[added + 2], refs[added + 3]
        ahead = pltpu.make_async_copy(grad_ref.at[:, pl.ds(following, next_ref.shape[1])], next_ref, sem)
        ahead.start()
    flat = len(out_ref.shape) - 1

    def columns(t, _):
        here = pl.ds(pl.multiple_of(t * step, 128), step)
        left = left_ref[spot].reshape(-1, depth)
        total = jnp.dot(left, right_ref[:, here], preferred_element_type=F32)
        total = total.reshape(*out_ref.shape[:-1], step)
        for n in range(added):
            total += refs[n][(*spot, slice(None), here)].astype(F32)
        total = total.astype(BF)
        if turned:
            for p in range(2):
                for q in range(2):
                    out_ref[q, p, :, here] = total[p, q]
        else:
            out_ref[(*(slice(None),) * flat, here)] = total
        return 0

    lax.fori_loop(0, out_ref.shape[-1] // step, columns, 0)
    if following is not None:
        ahead.wait()


def product(place, left, right, order=None, bit=0, add=None, grad=None, following=None):
    rows = left.shape[3]
    depth, width = right.shape
    dim = order[0] if order else None
    turned = bool(order) and order[1] > order[2]
    spot = tuple(bit if d == dim else slice(None) for d in range(3))
    kept = (2,) * (3 if dim is None else 2)
    args = [left, right] + ([] if add is None else [add])
    specs = [WHOLE] * len(args)
    args = [in_vmem(a) for a in args]
    outs = [pltpu.VMEM((*kept, rows, width), BF)]
    scratch = []
    if following is not None:
        column, follow_width, _ = CHUNKS[following]
        specs.append(pl.BlockSpec(memory_space=pltpu.HBM))
        args.append(in_hbm(grad))
        outs.append(pltpu.VMEM((depth, follow_width), BF))
        scratch.append(pltpu.SemaphoreType.DMA(()))
    else:
        column = None
    return pl.pallas_call(
        functools.partial(product_kernel, int(add is not None), column, spot, turned, width // 2),
        in_specs=[SCALARS] + specs,
        out_specs=[WHOLE] * len(outs),
        out_shape=outs,
        scratch_shapes=scratch,
        compiler_params=params(),
        cost_estimate=LIGHT,
        name="product",
    )(place, *args)


def adam_kernel(chained, column, group_column, place, *refs):
    mine_ref, came_ref, first_ref, second_ref, param_ref, anchor_ref, moment_ref = refs[:7]
    first_out, second_out = refs[7 + chained : 9 + chained]
    parts = refs[9 + chained : 13 + chained]
    quarters = refs[13 + chained]
    step = quarters.shape[-1]

    def columns(t, _):
        near = pl.ds(pl.multiple_of(t * step, 128), step)
        here = pl.ds(pl.multiple_of(column + t * step, 128), step)
        gradient = mine_ref[:, near].astype(F32) + came_ref[:, near].astype(F32)
        first_fresh = beta_first * first_ref[0, :, here].astype(F32) + (1.0 - beta_first) * gradient
        second_fresh = beta_second * second_ref[0, :, here].astype(F32) + (1.0 - beta_second) * gradient * gradient
        level = second_fresh * (1.0 / bias_second)
        root = level * lax.rsqrt(level)
        stepped = (1.0 - inner_rate * decay_rate) * param_ref[0, :, here]
        stepped = stepped - first_fresh * (inner_rate / bias_first) / (root + epsilon)
        first_out[0, :, here] = first_fresh.astype(BF)
        second_out[0, :, here] = second_fresh.astype(BF)
        departure = (anchor_ref[:, here] - stepped) * (pseudo_weight / REPLICAS) + moment_ref[:, here]
        quarters[...] = departure.reshape(quarters.shape)
        wide = pl.ds(pl.multiple_of(group_column + t * step, 128), step)
        for distance in range(4):
            parts[distance][:, wide] = quarters[place[1] ^ distance].astype(BF)
        return 0

    lax.fori_loop(0, mine_ref.shape[-1] // step, columns, 0)


def adam(place, grads, first, second, param, anchor, moment, column, width, before, group_column, group_width):
    rows, total_width = anchor.shape
    part = rows // 4
    part_shape = pltpu.VMEM((part, group_width), BF)
    firsts, seconds, parts = before
    chain = [(0, firsts), (1, seconds)] + [(2 + d, p) for d, p in enumerate(parts or ())]
    chain = [(o, a) for o, a in chain if a is not None]
    outs = pl.pallas_call(
        functools.partial(adam_kernel, len(chain), column, group_column),
        in_specs=[SCALARS] + [WHOLE] * (7 + len(chain)),
        out_specs=[WHOLE] * 6,
        scratch_shapes=[pltpu.VMEM((4, part, 128), F32)],
        out_shape=[pltpu.VMEM(first.shape, BF)] * 2 + [part_shape] * 4,
        input_output_aliases={8 + n: o for n, (o, _) in enumerate(chain)},
        compiler_params=params(),
        cost_estimate=LIGHT,
        name="adam",
    )(place, *(in_vmem(a) for a in (*grads, first, second, param, anchor, moment)), *(in_vmem(a) for _, a in chain))
    return outs[0], outs[1], outs[2:]


def hold_kernel(place, first, second, param, anchor, moment, *refs):
    outs, sems = refs[:5], refs[6]
    share_ref = refs[5]
    copies = [
        pltpu.make_async_copy(source, target, sems.at[n])
        for n, (source, target) in enumerate(zip((first, second, param, anchor, moment), (*outs[:4], share_ref)))
    ]
    for copy in copies:
        copy.start()
    placed = outs[4]
    width = share_ref.shape[1]
    placed[...] = jnp.zeros_like(placed)
    copies[4].wait()
    placed[:, pl.ds(pl.multiple_of(place[2] * width, 128), width)] = moment_weight * share_ref[...]
    for copy in copies[:4]:
        copy.wait()


def hold(place, first, second, param, anchor, moment):
    far = pl.BlockSpec(memory_space=pltpu.HBM)
    args = (first, second, param, anchor, moment)
    return pl.pallas_call(
        hold_kernel,
        in_specs=[SCALARS] + [far] * 5,
        out_specs=[WHOLE] * 5,
        out_shape=[pltpu.VMEM(a.shape, a.dtype) for a in args[:4]] + [pltpu.VMEM(anchor.shape, F32)],
        scratch_shapes=[pltpu.VMEM(moment.shape, F32), pltpu.SemaphoreType.DMA((5,))],
        compiler_params=params(),
        cost_estimate=LIGHT,
        name="hold",
    )(place, *(in_hbm(a) for a in args))


def store_kernel(place, first, second, part, first_out, second_out, part_out, sems):
    copies = [
        pltpu.make_async_copy(source, target, sems.at[n])
        for n, (source, target) in enumerate(((first, first_out), (second, second_out)))
    ]
    for copy in copies:
        copy.start()
    for copy in copies:
        copy.wait()


def store(place, first, second, part):
    far = pl.BlockSpec(memory_space=pltpu.HBM)
    return pl.pallas_call(
        store_kernel,
        in_specs=[SCALARS, WHOLE, WHOLE, WHOLE],
        out_specs=[far, far, WHOLE],
        out_shape=[pltpu.HBM(first.shape, BF)] * 2 + [pltpu.VMEM(part.shape, part.dtype)],
        scratch_shapes=[pltpu.SemaphoreType.DMA((2,))],
        input_output_aliases={3: 2},
        compiler_params=params(),
        cost_estimate=LIGHT,
        name="store",
    )(place, in_vmem(first), in_vmem(second), in_vmem(part))


def last_kernel(chained, final, column, place, p0, p1, p2, p3, anchor_ref, moment_ref, *refs):
    refs = refs[chained:]
    params_out, total_out = refs[:2]
    fresh, quarters, sems = refs[-3:]
    step = quarters.shape[-1]

    def columns(t, _):
        near = pl.ds(pl.multiple_of(t * step, 128), step)
        here = pl.ds(pl.multiple_of(column + t * step, 128), step)
        for distance, piece in enumerate((p0, p1, p2, p3)):
            quarters[place[1] ^ distance] = piece[:, near].astype(F32)
        total = quarters[...].reshape(-1, step)
        fresh[:, near] = anchor_ref[:, here] - outer_rate * total
        total_out[:, here] = total
        return 0

    lax.fori_loop(0, fresh.shape[-1] // step, columns, 0)
    copies = [pltpu.make_async_copy(fresh, params_out.at[:, pl.ds(column, fresh.shape[-1])], sems.at[0])]
    copies[0].start()
    if final:
        moment_out, moment = refs[2:4]
        width = moment.shape[-1]
        share = pl.ds(pl.multiple_of(place[2] * width, 128), width)
        weighted = moment_ref[:, share]
        pseudo = (total_out[:, share] - weighted) * (1.0 / pseudo_weight)
        moment[...] = weighted * (outer_beta / moment_weight) + pseudo
        copies.append(pltpu.make_async_copy(moment, moment_out, sems.at[1]))
        copies[1].start()
    for copy in copies:
        copy.wait()


def last(place, pieces, anchor, moment, column, width, before, share):
    rows = anchor.shape[0]
    chain = [a for a in before if a is not None]
    if chain:
        chain = [in_hbm(chain[0]), in_vmem(chain[1])]
    far = pl.BlockSpec(memory_space=pltpu.HBM)
    final = share is not None
    return pl.pallas_call(
        functools.partial(last_kernel, len(chain), final, column),
        in_specs=[SCALARS] + [WHOLE] * 6 + [far, WHOLE][: len(chain)],
        out_specs=[far, WHOLE] + [far] * final,
        out_shape=[pltpu.HBM(anchor.shape, F32), pltpu.VMEM(anchor.shape, F32)]
        + ([pltpu.HBM((rows, share), F32)] if final else []),
        scratch_shapes=([pltpu.VMEM((rows, share), F32)] if final else [])
        + [
            pltpu.VMEM((rows, width), F32),
            pltpu.VMEM((4, rows // 4, 128), F32),
            pltpu.SemaphoreType.DMA((2,)),
        ],
        input_output_aliases={7 + n: n for n in range(len(chain))},
        compiler_params=params(),
        cost_estimate=LIGHT,
        name="last",
    )(place, *(in_vmem(a) for a in (*pieces, anchor, moment)), *chain)


def add(*values):
    total = values[0].astype(F32)
    for value in values[1:]:
        total = total + value.astype(F32)
    return total.astype(BF)


def body(hidden, out_grad, inner_params, first_moment, second_moment, anchor, outer_moment):
    me = lax.axis_index("shard")
    rep = lax.axis_index("rep")
    place = jnp.stack([me, rep % 4, rep]).astype(jnp.int32)
    own, other, held = turn(hidden, out_grad, place)
    held = [held]
    count = len(CHUNKS)
    across, kept, arrived, twice, thrice = ([None] * count for _ in range(5))
    group_of = {n: g for g, group in enumerate(GROUPS) for n in group}
    parts, sums = [None] * len(GROUPS), [None] * len(GROUPS)
    firsts = seconds = None
    result = [None, None]
    token = place

    for kind, n in PLAN:
        column, width, order = CHUNKS[n]
        if kind == "other":
            following = n + 1 if n + 1 < count else None
            done, *more = product(token, other, held[n], grad=out_grad, following=following)
            held += more
            across[n] = swap(done, CORE)
        elif kind == "send":
            (done,) = product(token, own, held[n], order, 1, across[n])
            arrived[n] = swap(done, MASKS[order[0]])
        elif kind == "keep":
            (done,) = product(token, own, held[n], order, 0, across[n])
            kept[n] = done
        elif kind == "hold":
            first_held, second_held, param_held, anchor_held, moment_held = hold(
                token, first_moment, second_moment, inner_params, anchor, outer_moment
            )
            done = moment_held
        elif kind == "fold":
            mine, token = lax.optimization_barrier((kept[n], token))
            done = add(mine[1], arrived[n][1])
            twice[n] = (add(mine[0], arrived[n][0]), swap(done, MASKS[order[1]]))
        elif kind == "again":
            came = twice[n][1]
            mine, token = lax.optimization_barrier((twice[n][0], token))
            done = add(mine[1], came[1])
            thrice[n] = (add(mine[0], came[0]), swap(done, MASKS[order[2]]))
        elif kind == "adam":
            group = group_of[n]
            group_column = CHUNKS[GROUPS[group][0]][0]
            group_width = sum(CHUNKS[m][1] for m in GROUPS[group])
            firsts, seconds, parts[group] = adam(
                token, thrice[n], first_held, second_held, param_held, anchor_held, moment_held,
                column, width, (firsts, seconds, parts[group]), column - group_column, group_width,
            )
            done = parts[group][0]
            if n == GROUPS[group][-1]:
                parts[group] = [done] + [swap_rep(parts[group][d], d) for d in (1, 2, 3)]
        elif kind == "store":
            firsts, seconds, done = store(token, firsts, seconds, parts[n][0])
            parts[n][0] = done
        elif kind == "sum":
            mine, token = lax.optimization_barrier((parts[n][0], token))
            done = add(mine, *parts[n][1:])
            sums[n] = (done, swap_rep(done, 4))
        elif kind == "total":
            mine, token = lax.optimization_barrier((sums[n][0], token))
            done = add(mine, sums[n][1])
            sums[n] = [done] + [swap_rep(done, d) for d in (1, 2, 3)]
        elif kind == "last":
            column = CHUNKS[GROUPS[n][0]][0]
            width = sum(CHUNKS[m][1] for m in GROUPS[n])
            share = outer_moment.shape[1] if n == len(GROUPS) - 1 else None
            result = last(token, sums[n], anchor_held, moment_held, column, width, result, share)
            done = result[1]
        token, _ = lax.optimization_barrier((token, done))
    params_new, _, moment_new = result
    return (params_new, firsts, seconds, moment_new)


def solution(mesh):
    placed = (
        P(("rep", "shard"), None),
        P(("rep", "shard"), None),
        P("rep", "shard", None),
        P("rep", "shard", None),
        P("rep", "shard", None),
        P("shard", None),
        P("shard", "rep"),
    )
    return jax.shard_map(
        body,
        mesh=mesh,
        in_specs=placed,
        out_specs=(
            P("shard", None),
            P("rep", "shard", None),
            P("rep", "shard", None),
            P("shard", "rep"),
        ),
        check_vma=False,
    )
```
